32 devices in a mesh: dp: 2 (over x), seq: 4 (over y, core), fsdp: 4 (over z).
Axes of the slice: x: 2, y: 2, z: 4, core: 2. Of those that a mesh axis runs over, the one named last changes fastest.
Arguments:
- tokens: bfloat16 [8, 1024, 1024], P(('dp', 'fsdp'), 'seq'), may hold values from -6 to 6
- out_grad: bfloat16 [8, 1024, 1024], P(('dp', 'fsdp'), 'seq'), may hold values from -6 to 6
- doc_lengths: int32 [8, 4], P(('dp', 'fsdp')), may hold values from 1 to 896, as said below
- positions: int32 [8, 1024], P(('dp', 'fsdp'), 'seq'), may hold values from 0 to 2685, as said below
- norm1_gain: bfloat16 [1024], P(('dp', 'seq', 'fsdp')), may hold values from 0.5 to 1.5
- w_query: bfloat16 [1024, 1024], P(('dp', 'seq', 'fsdp')), may hold values from -0.1875 to 0.1875
- key_weight: bfloat16 [1024, 512], P(('dp', 'seq', 'fsdp')), may hold values from -0.1875 to 0.1875
- value_weight: bfloat16 [1024, 512], P(('dp', 'seq', 'fsdp')), may hold values from -0.1875 to 0.1875
- w_out: bfloat16 [1024, 1024], P(('dp', 'seq', 'fsdp')), may hold values from -3 to 3
- q_gain: bfloat16 [64], replicated, may hold values from 0.25 to 1.75
- k_gain: bfloat16 [64], replicated, may hold values from 0.25 to 1.75
- norm2_gain: bfloat16 [1024], P(('dp', 'seq', 'fsdp')), may hold values from 0.5 to 1.5
- w_gate: bfloat16 [1024, 4608], P(('dp', 'seq', 'fsdp')), may hold values from -0.1875 to 0.1875
- w_up: bfloat16 [1024, 4608], P(('dp', 'seq', 'fsdp')), may hold values from -0.1875 to 0.1875
- w_down: bfloat16 [4608, 1024], P(('dp', 'seq', 'fsdp')), may hold values from -0.09375 to 0.09375
Outputs:
- block_out: bfloat16 [8, 1024, 1024], P(('dp', 'fsdp'), 'seq')
- input_grad: bfloat16 [8, 1024, 1024], P(('dp', 'fsdp'), 'seq')
- grad_norm1: float32 [1024], P(('dp', 'seq', 'fsdp'))
- grad_query: float32 [1024, 1024], P(('dp', 'seq', 'fsdp'))
- grad_key: float32 [1024, 512], P(('dp', 'seq', 'fsdp'))
- grad_value: float32 [1024, 512], P(('dp', 'seq', 'fsdp'))
- grad_out: float32 [1024, 1024], P(('dp', 'seq', 'fsdp'))
- grad_q_gain: float32 [64], replicated
- grad_k_gain: float32 [64], replicated
- grad_norm2: float32 [1024], P(('dp', 'seq', 'fsdp'))
- grad_gate: float32 [1024, 4608], P(('dp', 'seq', 'fsdp'))
- grad_up: float32 [1024, 4608], P(('dp', 'seq', 'fsdp'))
- grad_down: float32 [4608, 1024], P(('dp', 'seq', 'fsdp'))
The draws below stay inside these ranges and needn't reach their ends.
Inputs may be any that keep to these rules, and one draw needn't show every extreme that they name: `doc_lengths`: each sequence holds 4 documents, in order, whose lengths sum to 1024; the longest has exactly 896 tokens. `positions`: positions start at 0 at each document's first token and rise by a fixed step of 1 to 3 per token within a document; the longest document's step is 3.
All inputs are finite; a program needn't handle non-finite values.
Results may differ from the reference program's by a relative error of at most 0.019.
Values may be sent and summed in bfloat16 or wider, within the bound.
A program may use at most 256 MiB of HBM per device.

```python
import jax
import jax.numpy as jnp
from jax import lax

MODEL_WIDTH = 1024
QUERY_HEADS = 16
KEY_VALUE_HEADS = 8
HEAD_SIZE = 64
FF = 4608
BLK = 256
DOCS = 4
SEQ = 1024
SEQS = 8


def document_plan(key):
    longest = 3 * BLK + BLK // 2
    remain = SEQ - longest

    def one_sequence(subkey):
        cut_key, order_key = jax.random.split(subkey)
        chosen = jax.random.permutation(cut_key, remain - 1)[:DOCS - 2] + 1
        cut_points = jnp.sort(chosen).astype(jnp.int32)
        bounds = jnp.concatenate([jnp.zeros((1,), jnp.int32), cut_points, jnp.full((1,), remain, jnp.int32)])
        smaller = bounds[1:] - bounds[:-1]
        lengths = jnp.concatenate([jnp.full((1,), longest, jnp.int32), smaller])
        return lengths[jax.random.permutation(order_key, DOCS)].astype(jnp.int32)
    return jax.vmap(one_sequence)(jax.random.split(key, SEQS))


def draw_doc_lengths(key, part):
    lengths = document_plan(key)
    return lengths


def draw_positions(key, part):
    lengths = document_plan(key)
    key = jax.random.fold_in(key, 23)
    doc_steps = jax.random.randint(key, (SEQS, DOCS), 1, 4, dtype=jnp.int32)

    def one_sequence(lengths_row, steps_row):
        longest_doc = jnp.argmax(lengths_row).astype(jnp.int32)
        steps_row = jnp.where(jnp.arange(DOCS, dtype=jnp.int32) == longest_doc, 3, steps_row).astype(jnp.int32)
        doc_ends = jnp.cumsum(lengths_row).astype(jnp.int32)
        starts = doc_ends - lengths_row
        indices = jnp.arange(SEQ, dtype=jnp.int32)
        segment = jnp.sum((indices[:, None] >= doc_ends[None, :]).astype(jnp.int32), axis=1)
        within = indices - starts[segment]
        return (within * steps_row[segment]).astype(jnp.int32)
    return jax.vmap(one_sequence)(lengths, doc_steps)


def raised(array, rng, source, target, parts, factor):
    def block_of(axis_at):
        return (jnp.arange(array.shape[axis_at]) // (array.shape[axis_at] // parts)).reshape((-1,) + (1,) * (array.ndim - 1 - axis_at))

    first = jax.random.permutation(rng, parts)[block_of(target)]
    second = (block_of(target) + parts // 2) % parts
    return jnp.where((block_of(source) == first) | (block_of(source) == second), factor * array, array)


def steps_of(key, extent, shards, least, top_value):
    loudness, own = 1.0, jax.random.fold_in(key, 6)
    for axis_at, shards_of in shards:
        heights = jnp.exp(jax.random.uniform(jax.random.fold_in(own, axis_at), (shards_of,), jnp.float32, least / len(shards), top_value / len(shards)))
        loudness = loudness * jnp.repeat(heights, extent[axis_at] // shards_of).reshape([-1 if axis == axis_at else 1 for axis in range(len(extent))])
    return loudness


def gaussian(stream_key, shape, spread, reach, pieces=(), held_as=jnp.bfloat16):
    values = spread * jax.random.normal(stream_key, shape, jnp.float32)
    if pieces:
        values = values * steps_of(stream_key, shape, pieces, -0.22, 0.18)
    return jnp.clip(values, -reach, reach).astype(held_as)


def noise_with(rng, extent, deviation, bound, pieces, heavy, kind=jnp.bfloat16):
    values = deviation * jax.random.normal(rng, extent, jnp.float32)
    if pieces:
        values = values * steps_of(rng, extent, pieces, -0.22, 0.18)
    return jnp.clip(raised(values, jax.random.fold_in(rng, 3), *heavy), -bound, bound).astype(kind)


def setup_inputs(seed: int = 0) -> dict:
    keys = jax.random.split(jax.random.key(seed), 16)
    tokens = noise_with(keys[0], (SEQS, SEQ, MODEL_WIDTH), 1.0, 6.0, ((0, 8), (1, 4)), (0, 2, 8, 2.0))
    out_grad = gaussian(keys[1], (SEQS, SEQ, MODEL_WIDTH), 1.0, 6.0, ((0, 8), (1, 4)))
    doc_lengths = draw_doc_lengths(jax.random.fold_in(keys[15], 71), 0)
    positions = draw_positions(jax.random.fold_in(keys[15], 71), 0)
    norm1_gain = jnp.clip(1.0 + 0.1 * jax.random.normal(keys[4], (MODEL_WIDTH,), jnp.float32), 0.5, 1.5).astype(jnp.bfloat16)
    w_query = gaussian(keys[5], (MODEL_WIDTH, QUERY_HEADS * HEAD_SIZE), MODEL_WIDTH ** -0.5, 0.1875, ((0, 32),))
    key_weight = gaussian(keys[6], (MODEL_WIDTH, KEY_VALUE_HEADS * HEAD_SIZE), MODEL_WIDTH ** -0.5, 0.1875, ((0, 32),))
    value_weight = gaussian(keys[7], (MODEL_WIDTH, KEY_VALUE_HEADS * HEAD_SIZE), MODEL_WIDTH ** -0.5, 0.1875, ((0, 32),))
    w_out = gaussian(keys[8], (QUERY_HEADS * HEAD_SIZE, MODEL_WIDTH), (max(QUERY_HEADS * HEAD_SIZE // 256, 4)) ** -0.5, 3.0, ((0, 32),))
    q_gain = jnp.clip(1.0 + 0.15 * jax.random.normal(keys[9], (HEAD_SIZE,), jnp.float32), 0.25, 1.75).astype(jnp.bfloat16)
    k_gain = jnp.clip(1.0 + 0.15 * jax.random.normal(keys[10], (HEAD_SIZE,), jnp.float32), 0.25, 1.75).astype(jnp.bfloat16)
    norm2_gain = jnp.clip(1.0 + 0.1 * jax.random.normal(keys[11], (MODEL_WIDTH,), jnp.float32), 0.5, 1.5).astype(jnp.bfloat16)
    w_gate = gaussian(keys[12], (MODEL_WIDTH, FF), MODEL_WIDTH ** -0.5, 0.1875, ((0, 32),))
    w_up = gaussian(keys[13], (MODEL_WIDTH, FF), MODEL_WIDTH ** -0.5, 0.1875, ((0, 32),))
    w_down = gaussian(keys[14], (FF, MODEL_WIDTH), FF ** -0.5, 0.09375, ((0, 32),))
    return dict(tokens=tokens, out_grad=out_grad, doc_lengths=doc_lengths, positions=positions, norm1_gain=norm1_gain, w_query=w_query, key_weight=key_weight, value_weight=value_weight, w_out=w_out, q_gain=q_gain, k_gain=k_gain, norm2_gain=norm2_gain, w_gate=w_gate, w_up=w_up, w_down=w_down)


epsilon = 1e-05
rope_base = 1000000.0
score_scale = 0.125
masked_fill_value = -1e+30
highest = lax.Precision.HIGHEST

@jax.custom_vjp
def low(v):
    return lax.optimization_barrier(v.astype(jnp.bfloat16)).astype(jnp.float32)

@jax.custom_vjp
def low_back(v):
    return v

def low_keep(v):
    return (low(v), None)

def low_pass(kept, grad):
    return (grad,)

def back_keep(v):
    return (v, None)

def back_low(kept, grad):
    return (low(grad),)
low.defvjp(low_keep, low_pass)
low_back.defvjp(back_keep, back_low)

def matmul(left, right):
    return jnp.dot(left, right, precision=highest, preferred_element_type=jnp.float32)

def rms_scale(value_rows, norm_gain):
    return value_rows * lax.rsqrt(lax.optimization_barrier(jnp.mean(value_rows * value_rows, axis=-1, keepdims=True)) + epsilon) * norm_gain

def rotary_tables(position):
    half_width = HEAD_SIZE // 2
    freqs = rope_base ** (-2.0 * jnp.arange(half_width, dtype=jnp.float32) / HEAD_SIZE)
    angles = position.astype(jnp.float32)[:, None] * freqs[None, :]
    angles = jnp.concatenate([angles, angles], axis=1)
    return (jnp.cos(angles), jnp.sin(angles))

def head_norm_rotary(unnormed_rows, norm_gain, cosine_table, sine_table, heads):
    token_rows = unnormed_rows.shape[0]
    split_rows = unnormed_rows.reshape(token_rows, heads, HEAD_SIZE)
    normed = rms_scale(split_rows, norm_gain)
    first_half = normed[..., :HEAD_SIZE // 2]
    second_half = normed[..., HEAD_SIZE // 2:]
    turned = jnp.concatenate([-second_half, first_half], axis=-1)
    rotated = normed * cosine_table[:, None, :] + turned * sine_table[:, None, :]
    return rotated.reshape(token_rows, heads * HEAD_SIZE)

def segment_ids(lengths, length_all):
    doc_ends = jnp.cumsum(lengths).astype(jnp.int32)
    indices = jnp.arange(length_all, dtype=jnp.int32)
    return lax.optimization_barrier(jnp.sum((indices[:, None] >= doc_ends[None, :]).astype(jnp.int32), axis=1))

def forward(inputs, weights, segments, cosine_table, sine_table):
    gain_one, w_q, w_k, w_v, w_o, gain_q, key_norm_gain, gain_two, w_g, w_u, w_d = weights
    token_rows = inputs.shape[0]
    queries_per_group = QUERY_HEADS // KEY_VALUE_HEADS
    normed1 = low(rms_scale(inputs, gain_one))
    query_raw = low_back(matmul(normed1, w_q))
    key_unnormed = low_back(matmul(normed1, w_k))
    value_raw = low_back(matmul(normed1, w_v))
    query_rows = low(low_back(head_norm_rotary(query_raw, gain_q, cosine_table, sine_table, QUERY_HEADS)))
    key_rows = low(low_back(head_norm_rotary(key_unnormed, key_norm_gain, cosine_table, sine_table, KEY_VALUE_HEADS)))
    value_rows = low(value_raw)
    query_heads = query_rows.reshape(token_rows, QUERY_HEADS, HEAD_SIZE).transpose(1, 0, 2)
    heads_of_key = jnp.repeat(key_rows.reshape(token_rows, KEY_VALUE_HEADS, HEAD_SIZE).transpose(1, 0, 2), queries_per_group, axis=0)
    heads_of_value = jnp.repeat(value_rows.reshape(token_rows, KEY_VALUE_HEADS, HEAD_SIZE).transpose(1, 0, 2), queries_per_group, axis=0)
    indices = jnp.arange(token_rows, dtype=jnp.int32)
    allowed = (segments[:, None] == segments[None, :]) & (indices[:, None] >= indices[None, :])

    def one_head(head_block):
        head_q, head_k, head_v = head_block
        scores = low_back(matmul(head_q, head_k.T) * score_scale)
        scores = jnp.where(allowed, scores, masked_fill_value)
        row_top = lax.optimization_barrier(jnp.max(scores, axis=1, keepdims=True))
        expo = jnp.exp(scores - row_top)
        probs = expo / lax.optimization_barrier(jnp.sum(expo, axis=1, keepdims=True))
        return matmul(low(probs), head_v)
    head_outs = lax.map(jax.checkpoint(one_head), (query_heads, heads_of_key, heads_of_value))
    attended = head_outs.transpose(1, 0, 2).reshape(token_rows, QUERY_HEADS * HEAD_SIZE)
    attended = low(low_back(attended))
    middle = inputs + low_back(matmul(attended, w_o))
    normed2 = low(rms_scale(middle, gain_two))
    gate_pre = low_back(matmul(normed2, w_g))
    up_pre = low_back(matmul(normed2, w_u))
    hidden = low(jax.nn.silu(gate_pre) * up_pre)
    return middle + low_back(matmul(hidden, w_d))

def reference(tokens, out_grad, doc_lengths, positions, norm1_gain, w_query, key_weight, value_weight, w_out, q_gain, k_gain, norm2_gain, w_gate, w_up, w_down):
    params = tuple((weight_arg.astype(jnp.float32) for weight_arg in (norm1_gain, w_query, key_weight, value_weight, w_out, q_gain, k_gain, norm2_gain, w_gate, w_up, w_down)))
    seq_len = tokens.shape[1]

    def per_sequence(running, sequence_in):
        inputs, cotangent, lengths, position = sequence_in
        segments = segment_ids(lengths, seq_len)
        cosine_table, sine_table = rotary_tables(position)

        def layer_fn(inputs_f, *weights):
            return forward(inputs_f, weights, segments, cosine_table, sine_table)
        result, pullback = jax.vjp(layer_fn, inputs.astype(jnp.float32), *params)
        gradients = pullback(cotangent.astype(jnp.float32))
        running = tuple((before + update for before, update in zip(running, gradients[1:])))
        return (running, (result.astype(jnp.bfloat16), gradients[0].astype(jnp.bfloat16)))
    zeros_init = tuple((jnp.zeros(weight_arg.shape, jnp.float32) for weight_arg in params))
    totals, (block_out, input_grad) = lax.scan(per_sequence, zeros_init, (tokens, out_grad, doc_lengths, positions))
    return (block_out, input_grad, totals[0], totals[1], totals[2], totals[3], totals[4], totals[5], totals[6], totals[7], totals[8], totals[9], totals[10])
```

```python
import jax
import jax.numpy as jnp
from jax import lax
from jax.sharding import PartitionSpec as P

MODEL_WIDTH = 1024
QUERY_HEADS = 16
KEY_VALUE_HEADS = 8
HEAD_SIZE = 64
FF = 4608


epsilon = 1e-05
rope_base = 1000000.0
score_scale = 0.125
masked_fill_value = -1e30


def rms_scale(value_rows, norm_gain):
    return (
        value_rows
        * lax.rsqrt(jnp.mean(value_rows * value_rows, axis=-1, keepdims=True) + epsilon)
        * norm_gain
    )


def rotary_tables(position):
    half_width = HEAD_SIZE // 2
    freqs = rope_base ** (-2.0 * jnp.arange(half_width, dtype=jnp.float32) / HEAD_SIZE)
    angles = position.astype(jnp.float32)[:, None] * freqs[None, :]
    angles = jnp.concatenate([angles, angles], axis=1)
    return (jnp.cos(angles), jnp.sin(angles))


def head_norm_rotary(unnormed_rows, norm_gain, cosine_table, sine_table, heads):
    token_rows = unnormed_rows.shape[0]
    split_rows = unnormed_rows.reshape(token_rows, heads, HEAD_SIZE)
    normed = rms_scale(split_rows, norm_gain)
    first_half = normed[..., : HEAD_SIZE // 2]
    second_half = normed[..., HEAD_SIZE // 2 :]
    turned = jnp.concatenate([-second_half, first_half], axis=-1)
    rotated = normed * cosine_table[:, None, :] + turned * sine_table[:, None, :]
    return rotated.reshape(token_rows, heads * HEAD_SIZE)


def segment_ids(lengths, length_all):
    doc_ends = jnp.cumsum(lengths)
    indices = jnp.arange(length_all, dtype=jnp.int32)
    return jnp.sum((indices[:, None] >= doc_ends[None, :]).astype(jnp.int32), axis=1)


def rounded(value_rows):
    return lax.optimization_barrier(value_rows.astype(jnp.bfloat16)).astype(jnp.float32)


def matmul(left, right):
    return jnp.dot(left, right, preferred_element_type=jnp.float32)


def contract_rows(left, right):
    return lax.dot_general(
        left, right, (((0,), (0,)), ((), ())), preferred_element_type=jnp.float32
    )


def contract_cols(left, right):
    return lax.dot_general(
        left, right, (((1,), (1,)), ((), ())), preferred_element_type=jnp.float32
    )


def column_term(left, right):
    return contract_rows(left, right)


def body(
    tokens,
    out_grad,
    doc_lengths,
    positions,
    norm1_gain,
    w_query,
    key_weight,
    value_weight,
    w_out,
    q_gain,
    k_gain,
    norm2_gain,
    w_gate,
    w_up,
    w_down,
):
    token_rows = tokens.shape[1]
    seq_parts = lax.axis_size("seq")
    my_index = lax.axis_index("seq")
    seq_len = token_rows * seq_parts
    queries_per_group = QUERY_HEADS // KEY_VALUE_HEADS
    segments = segment_ids(doc_lengths[0], seq_len)
    own_offset = my_index * token_rows
    own_segments = lax.dynamic_slice_in_dim(segments, own_offset, token_rows)
    own_places = own_offset + jnp.arange(token_rows, dtype=jnp.int32)
    cosine_table, sine_table = rotary_tables(positions[0])
    weight_rows = w_query.shape[0]
    query_cols = QUERY_HEADS * HEAD_SIZE
    kv_cols = KEY_VALUE_HEADS * HEAD_SIZE
    qkv_cols = query_cols + 2 * kv_cols
    packed = jnp.concatenate(
        [
            w_query,
            key_weight,
            value_weight,
            w_out,
            norm1_gain[:, None],
            norm2_gain[:, None],
            jnp.zeros((weight_rows, 126), jnp.bfloat16),
        ],
        axis=1,
    )
    packed = lax.all_gather(packed, ("dp", "seq", "fsdp"), axis=0, tiled=True)
    qkv_all = packed[:, :qkv_cols]
    out_all = packed[:, qkv_cols : qkv_cols + MODEL_WIDTH]
    norm1_all = packed[:, qkv_cols + MODEL_WIDTH]
    norm2_all = packed[:, qkv_cols + MODEL_WIDTH + 1]

    dp_parts = lax.axis_size("dp")
    fsdp_parts = lax.axis_size("fsdp")
    unit_rows = w_down.shape[0]
    units = dp_parts * fsdp_parts * unit_rows

    def by_owner(columns):
        split = columns.reshape(weight_rows, dp_parts, seq_parts, fsdp_parts, unit_rows)
        return split.transpose(2, 0, 1, 3, 4).reshape(seq_parts, weight_rows, units)

    gate_up = jnp.concatenate([by_owner(w_gate), by_owner(w_up)], axis=2)
    gate_up = lax.all_to_all(gate_up, "seq", 0, 0)
    gate_up = lax.all_gather(
        gate_up.reshape(seq_parts * weight_rows, 2 * units), ("dp", "fsdp"), axis=0, tiled=True
    )
    gate_up = (
        gate_up.reshape(dp_parts, fsdp_parts, seq_parts, weight_rows, 2 * units)
        .transpose(0, 2, 1, 3, 4)
        .reshape(MODEL_WIDTH, 2 * units)
    )
    down_all = lax.all_gather(w_down, ("dp", "fsdp"), axis=0, tiled=True)
    grad_all = lax.all_gather(out_grad[0], "seq", axis=0, tiled=True)
    inputs = tokens[0].astype(jnp.float32)
    gain_one = norm1_all.astype(jnp.float32)
    normed1 = rms_scale(inputs, gain_one).astype(jnp.bfloat16)
    qkv_raw = matmul(normed1, qkv_all)
    query_raw = qkv_raw[:, :query_cols]
    key_unnormed = qkv_raw[:, query_cols : query_cols + kv_cols]
    value_raw = qkv_raw[:, query_cols + kv_cols :]
    gain_query = q_gain.astype(jnp.float32)
    gain_key = k_gain.astype(jnp.float32)

    def query_part(unnormed_rows, norm_gain):
        return head_norm_rotary(unnormed_rows, norm_gain, cosine_table, sine_table, QUERY_HEADS)

    def key_part(unnormed_rows, norm_gain):
        return head_norm_rotary(unnormed_rows, norm_gain, cosine_table, sine_table, KEY_VALUE_HEADS)

    query_rows = query_part(query_raw, gain_query).astype(jnp.bfloat16)
    key_rows = key_part(key_unnormed, gain_key).astype(jnp.bfloat16)
    value_rows = value_raw.astype(jnp.bfloat16)
    query_four_axes = query_rows.reshape(token_rows, KEY_VALUE_HEADS, queries_per_group, HEAD_SIZE)

    def scores_for(key_rows_part):
        total_amount = key_rows_part.shape[0]
        key_three_axes = key_rows_part.reshape(total_amount, KEY_VALUE_HEADS, HEAD_SIZE)
        scores = (
            jnp.einsum(
                "qhgd,khd->hgqk",
                query_four_axes,
                key_three_axes,
                preferred_element_type=jnp.float32,
            )
            * score_scale
        )
        key_places = jnp.arange(total_amount, dtype=jnp.int32)
        allowed = (own_segments[:, None] == segments[None, :]) & (
            own_places[:, None] >= key_places[None, :]
        )
        return (scores, allowed, key_three_axes)

    starting_maximum = jnp.full(
        (KEY_VALUE_HEADS, queries_per_group, token_rows), masked_fill_value, jnp.float32
    )
    row_top = starting_maximum
    both_rows = lax.all_gather(
        jnp.concatenate([key_rows, value_rows], axis=1), "seq", axis=0, tiled=True
    )
    key_rows_part = both_rows[:, :kv_cols]
    value_rows_part = both_rows[:, kv_cols:]
    total_amount = key_rows_part.shape[0]
    scores, allowed, key_three_axes = scores_for(key_rows_part)
    masked = jnp.where(allowed, scores, masked_fill_value)
    new_top = jnp.maximum(row_top, jnp.max(masked, axis=-1))
    expo = jnp.where(allowed, jnp.exp(masked - new_top[..., None]), 0.0)
    row_sum = jnp.sum(expo, axis=-1)
    value_three_axes = value_rows_part.reshape(total_amount, KEY_VALUE_HEADS, HEAD_SIZE)
    summed = jnp.einsum(
        "hgqk,khd->hgqd",
        expo.astype(jnp.bfloat16),
        value_three_axes,
        preferred_element_type=jnp.float32,
    )
    row_top, row_sum, summed = (new_top, row_sum, summed)
    attended = summed / row_sum[..., None]
    log_total = row_top + jnp.log(row_sum)
    attended_b = (
        attended.transpose(2, 0, 1, 3)
        .reshape(token_rows, QUERY_HEADS * HEAD_SIZE)
        .astype(jnp.bfloat16)
    )
    middle = inputs + matmul(attended_b, out_all)
    gain_two = norm2_all.astype(jnp.float32)
    normed2 = rms_scale(middle, gain_two).astype(jnp.bfloat16)
    normed2_all = lax.all_gather(normed2, "seq", axis=0, tiled=True)
    gate_up_pre = matmul(normed2_all, gate_up)
    gate_pre = gate_up_pre[:, :units]
    up_pre = gate_up_pre[:, units:]

    def swiglu(gate_in, up_in):
        return jax.nn.silu(gate_in) * up_in

    swiglu_out, swiglu_pull = jax.vjp(swiglu, gate_pre, up_pre)
    hidden = swiglu_out.astype(jnp.bfloat16)
    d_hidden = contract_cols(grad_all, down_all)
    d_gate, d_up = swiglu_pull(d_hidden)
    gate_up_grads = jnp.concatenate([d_gate.astype(jnp.bfloat16), d_up.astype(jnp.bfloat16)], axis=1)
    d_normed2 = contract_cols(gate_up_grads, gate_up).astype(jnp.bfloat16)
    d_normed2 = lax.psum_scatter(d_normed2, "seq", scatter_dimension=0, tiled=True)
    d_normed2 = d_normed2.astype(jnp.float32)
    branch = lax.psum_scatter(
        matmul(hidden, down_all).astype(jnp.bfloat16), "seq", scatter_dimension=0, tiled=True
    )
    block_out = (middle + branch.astype(jnp.float32)).astype(jnp.bfloat16)
    down_sum = lax.psum_scatter(
        column_term(hidden, grad_all).astype(jnp.bfloat16),
        ("dp", "fsdp"),
        scatter_dimension=0,
        tiled=True,
    ).astype(jnp.float32)
    gate_up_sum = (
        column_term(normed2_all, gate_up_grads)
        .astype(jnp.bfloat16)
        .reshape(dp_parts, seq_parts, fsdp_parts, weight_rows, 2 * units)
        .transpose(0, 2, 1, 3, 4)
        .reshape(MODEL_WIDTH, 2 * units)
    )
    gate_up_sum = lax.psum_scatter(gate_up_sum, ("dp", "fsdp"), scatter_dimension=0, tiled=True)
    gate_up_sum = lax.all_to_all(
        gate_up_sum.reshape(seq_parts, weight_rows, 2 * units), "seq", 0, 0
    )

    def to_columns(owned):
        split = owned.reshape(seq_parts, weight_rows, dp_parts, fsdp_parts, unit_rows)
        return split.transpose(1, 2, 0, 3, 4).reshape(weight_rows, FF).astype(jnp.float32)

    grad_gate = to_columns(gate_up_sum[:, :, :units])
    grad_up = to_columns(gate_up_sum[:, :, units:])
    grad_rows = out_grad[0]
    grad_float = grad_rows.astype(jnp.float32)
    norm2_out, norm2_pull = jax.vjp(rms_scale, middle, gain_two)
    d_middle_norm, d_gain_two = norm2_pull(d_normed2)
    d_middle = grad_float + d_middle_norm
    d_branch = d_middle.astype(jnp.bfloat16)
    out_sum = lax.psum_scatter(
        column_term(attended_b, d_branch).astype(jnp.bfloat16),
        ("dp", "seq", "fsdp"),
        scatter_dimension=0,
        tiled=True,
    ).astype(jnp.float32)
    attended_gradient = contract_cols(d_branch, out_all).astype(jnp.bfloat16)
    attended_grad_four = attended_gradient.reshape(
        token_rows, KEY_VALUE_HEADS, queries_per_group, HEAD_SIZE
    ).transpose(1, 2, 0, 3)
    delta_rows = jnp.sum(attended_grad_four.astype(jnp.float32) * attended, axis=-1)
    scores, allowed, key_three_axes = scores_for(key_rows_part)
    probs = jnp.where(allowed, jnp.exp(scores - log_total[..., None]), 0.0)
    value_three_axes = value_rows_part.reshape(total_amount, KEY_VALUE_HEADS, HEAD_SIZE)
    value_gradient = jnp.einsum(
        "hgqk,hgqd->khd",
        probs.astype(jnp.bfloat16),
        attended_grad_four,
        preferred_element_type=jnp.float32,
    )
    d_probs = jnp.einsum(
        "hgqd,khd->hgqk", attended_grad_four, value_three_axes, preferred_element_type=jnp.float32
    )
    d_scores = (probs * (d_probs - delta_rows[..., None])).astype(jnp.bfloat16)
    d_query_acc = (
        jnp.einsum("hgqk,khd->hgqd", d_scores, key_three_axes, preferred_element_type=jnp.float32)
        * score_scale
    )
    local_key_gradient = (
        jnp.einsum("hgqk,qhgd->khd", d_scores, query_four_axes, preferred_element_type=jnp.float32)
        * score_scale
    )
    every_key_gradient = local_key_gradient.reshape(total_amount, KEY_VALUE_HEADS * HEAD_SIZE)
    every_value_gradient = value_gradient.reshape(total_amount, KEY_VALUE_HEADS * HEAD_SIZE)
    d_both_own = lax.psum_scatter(
        jnp.concatenate([every_key_gradient, every_value_gradient], axis=1).astype(jnp.bfloat16),
        "seq",
        scatter_dimension=0,
        tiled=True,
    )
    d_keys_own = d_both_own[:, :kv_cols].astype(jnp.float32)
    d_values_own = d_both_own[:, kv_cols:]
    d_query_rows = rounded(
        d_query_acc.transpose(2, 0, 1, 3).reshape(token_rows, QUERY_HEADS * HEAD_SIZE)
    )
    query_out, query_pull = jax.vjp(query_part, query_raw, gain_query)
    d_query_raw, d_gain_query = query_pull(d_query_rows)
    key_out, key_pull = jax.vjp(key_part, key_unnormed, gain_key)
    d_key_raw, d_gain_key = key_pull(d_keys_own)
    d_query_b = d_query_raw.astype(jnp.bfloat16)
    d_key_b = d_key_raw.astype(jnp.bfloat16)
    projection_grads = jnp.concatenate([d_query_b, d_key_b, d_values_own], axis=1)
    projection_sum = lax.psum_scatter(
        column_term(normed1, projection_grads).astype(jnp.bfloat16),
        ("dp", "seq", "fsdp"),
        scatter_dimension=0,
        tiled=True,
    ).astype(jnp.float32)
    d_normed1 = contract_cols(projection_grads, qkv_all)
    norm1_out, norm1_pull = jax.vjp(rms_scale, inputs, gain_one)
    d_input_norm, d_gain_one = norm1_pull(d_normed1)
    gain_sums = lax.psum((d_gain_one, d_gain_two, d_gain_query, d_gain_key), ("dp", "seq", "fsdp"))
    input_grad = (d_middle + d_input_norm).astype(jnp.bfloat16)
    width_share = weight_rows
    share_start = lax.axis_index(("dp", "seq", "fsdp")) * width_share
    gain_one_own = lax.dynamic_slice_in_dim(gain_sums[0], share_start, width_share)
    gain_two_own = lax.dynamic_slice_in_dim(gain_sums[1], share_start, width_share)
    grad_query = projection_sum[:, :query_cols]
    grad_key = projection_sum[:, query_cols : query_cols + kv_cols]
    grad_value = projection_sum[:, query_cols + kv_cols :]
    return (
        block_out[None],
        input_grad[None],
        gain_one_own,
        grad_query,
        grad_key,
        grad_value,
        out_sum,
        gain_sums[2],
        gain_sums[3],
        gain_two_own,
        grad_gate,
        grad_up,
        down_sum,
    )


def solution(mesh):
    in_specs = (
        P(("dp", "fsdp"), "seq", None),
        P(("dp", "fsdp"), "seq", None),
        P(("dp", "fsdp"), None),
        P(("dp", "fsdp"), "seq"),
        P(("dp", "seq", "fsdp")),
        P(("dp", "seq", "fsdp"), None),
        P(("dp", "seq", "fsdp"), None),
        P(("dp", "seq", "fsdp"), None),
        P(("dp", "seq", "fsdp"), None),
        P(),
        P(),
        P(("dp", "seq", "fsdp")),
        P(("dp", "seq", "fsdp"), None),
        P(("dp", "seq", "fsdp"), None),
        P(("dp", "seq", "fsdp"), None),
    )
    out_specs = (
        P(("dp", "fsdp"), "seq", None),
        P(("dp", "fsdp"), "seq", None),
        P(("dp", "seq", "fsdp")),
        P(("dp", "seq", "fsdp"), None),
        P(("dp", "seq", "fsdp"), None),
        P(("dp", "seq", "fsdp"), None),
        P(("dp", "seq", "fsdp"), None),
        P(),
        P(),
        P(("dp", "seq", "fsdp")),
        P(("dp", "seq", "fsdp"), None),
        P(("dp", "seq", "fsdp"), None),
        P(("dp", "seq", "fsdp"), None),
    )
    return jax.shard_map(body, mesh=mesh, in_specs=in_specs, out_specs=out_specs, check_vma=False)
```

```python
import jax
import jax.numpy as jnp
from jax import lax
from jax.sharding import PartitionSpec as P

MODEL_WIDTH = 1024
QUERY_HEADS = 16
KEY_VALUE_HEADS = 8
HEAD_SIZE = 64
FF = 4608


epsilon = 1e-05
rope_base = 1000000.0
score_scale = 0.125
masked_fill_value = -1e30


def rms_scale(value_rows, norm_gain):
    return (
        value_rows
        * lax.rsqrt(jnp.mean(value_rows * value_rows, axis=-1, keepdims=True) + epsilon)
        * norm_gain
    )


def rotary_tables(position):
    half_width = HEAD_SIZE // 2
    freqs = rope_base ** (-2.0 * jnp.arange(half_width, dtype=jnp.float32) / HEAD_SIZE)
    angles = position.astype(jnp.float32)[:, None] * freqs[None, :]
    angles = jnp.concatenate([angles, angles], axis=1)
    return (jnp.cos(angles), jnp.sin(angles))


def head_norm_rotary(unnormed_rows, norm_gain, cosine_table, sine_table, heads):
    token_rows = unnormed_rows.shape[0]
    split_rows = unnormed_rows.reshape(token_rows, heads, HEAD_SIZE)
    normed = rms_scale(split_rows, norm_gain)
    first_half = normed[..., : HEAD_SIZE // 2]
    second_half = normed[..., HEAD_SIZE // 2 :]
    turned = jnp.concatenate([-second_half, first_half], axis=-1)
    rotated = normed * cosine_table[:, None, :] + turned * sine_table[:, None, :]
    return rotated.reshape(token_rows, heads * HEAD_SIZE)


def segment_ids(lengths, length_all):
    doc_ends = jnp.cumsum(lengths)
    indices = jnp.arange(length_all, dtype=jnp.int32)
    return jnp.sum((indices[:, None] >= doc_ends[None, :]).astype(jnp.int32), axis=1)


def rounded(value_rows):
    return lax.optimization_barrier(value_rows.astype(jnp.bfloat16)).astype(jnp.float32)


def matmul(left, right):
    return jnp.dot(left, right, preferred_element_type=jnp.float32)


def contract_rows(left, right):
    return lax.dot_general(
        left, right, (((0,), (0,)), ((), ())), preferred_element_type=jnp.float32
    )


def contract_cols(left, right):
    return lax.dot_general(
        left, right, (((1,), (1,)), ((), ())), preferred_element_type=jnp.float32
    )


def exchange(blocks, bit, parts):
    pairs = [(place, place ^ bit) for place in range(parts)]
    received = lax.ppermute(jnp.concatenate(blocks, axis=0), "seq", pairs)
    return jnp.split(received, len(blocks), axis=0)


def gather_seq(own):
    parts = lax.axis_size("seq")
    blocks = {0: own}
    bit = parts // 2
    while bit:
        keys = sorted(blocks)
        for key, block in zip(keys, exchange([blocks[key] for key in keys], bit, parts)):
            blocks[key ^ bit] = block
        bit //= 2
    return [blocks[key] for key in range(parts)]


def scatter_seq(blocks):
    parts = lax.axis_size("seq")
    held = {key: block.astype(jnp.float32) for key, block in enumerate(blocks)}
    bit = 1
    while bit < parts:
        keys = [key for key in sorted(held) if key & bit]
        sent = [held.pop(key).astype(jnp.bfloat16) for key in keys]
        for key, block in zip(keys, exchange(sent, bit, parts)):
            held[key ^ bit] = held[key ^ bit] + block.astype(jnp.float32)
        bit *= 2
    return held[0]


def column_term(left, right):
    return contract_rows(left, right)


def body(
    tokens,
    out_grad,
    doc_lengths,
    positions,
    norm1_gain,
    w_query,
    key_weight,
    value_weight,
    w_out,
    q_gain,
    k_gain,
    norm2_gain,
    w_gate,
    w_up,
    w_down,
):
    token_rows = tokens.shape[1]
    seq_parts = lax.axis_size("seq")
    my_index = lax.axis_index("seq")
    seq_len = token_rows * seq_parts
    queries_per_group = QUERY_HEADS // KEY_VALUE_HEADS
    segments = segment_ids(doc_lengths[0], seq_len)
    own_offset = my_index * token_rows
    own_segments = lax.dynamic_slice_in_dim(segments, own_offset, token_rows)
    own_places = own_offset + jnp.arange(token_rows, dtype=jnp.int32)
    cosine_table, sine_table = rotary_tables(positions[0])
    weight_rows = w_query.shape[0]
    query_cols = QUERY_HEADS * HEAD_SIZE
    kv_cols = KEY_VALUE_HEADS * HEAD_SIZE
    qkv_cols = query_cols + 2 * kv_cols
    packed = jnp.concatenate(
        [
            w_query,
            key_weight,
            value_weight,
            w_out,
            norm1_gain[:, None],
            norm2_gain[:, None],
            jnp.zeros((weight_rows, 126), jnp.bfloat16),
        ],
        axis=1,
    )
    packed = lax.all_gather(packed, ("dp", "seq", "fsdp"), axis=0, tiled=True)

    dp_parts = lax.axis_size("dp")
    fsdp_parts = lax.axis_size("fsdp")
    unit_rows = w_down.shape[0]
    units = dp_parts * fsdp_parts * unit_rows

    def by_owner(columns):
        split = columns.reshape(weight_rows, dp_parts, seq_parts, fsdp_parts, unit_rows)
        return split.transpose(2, 0, 1, 3, 4).reshape(seq_parts, weight_rows, units)

    gate_up = jnp.concatenate([by_owner(w_gate), by_owner(w_up)], axis=2)
    gate_up = lax.all_to_all(gate_up, "seq", 0, 0)
    packed, gate_up = lax.optimization_barrier((packed, gate_up))
    qkv_all = packed[:, :qkv_cols]
    out_all = packed[:, qkv_cols : qkv_cols + MODEL_WIDTH]
    norm1_all = packed[:, qkv_cols + MODEL_WIDTH]
    norm2_all = packed[:, qkv_cols + MODEL_WIDTH + 1]
    gate_up = lax.all_gather(
        gate_up.reshape(seq_parts * weight_rows, 2 * units), ("dp", "fsdp"), axis=0, tiled=True
    )
    gate_up = (
        gate_up.reshape(dp_parts, fsdp_parts, seq_parts, weight_rows, 2 * units)
        .transpose(0, 2, 1, 3, 4)
        .reshape(MODEL_WIDTH, 2 * units)
    )
    down_all = lax.all_gather(w_down, ("dp", "fsdp"), axis=0, tiled=True)
    grad_all = jnp.concatenate(gather_seq(out_grad[0]), axis=0)
    inputs = tokens[0].astype(jnp.float32)
    gain_one = norm1_all.astype(jnp.float32)
    normed1 = rms_scale(inputs, gain_one).astype(jnp.bfloat16)
    qkv_raw = matmul(normed1, qkv_all)
    query_raw = qkv_raw[:, :query_cols]
    key_unnormed = qkv_raw[:, query_cols : query_cols + kv_cols]
    value_raw = qkv_raw[:, query_cols + kv_cols :]
    gain_query = q_gain.astype(jnp.float32)
    gain_key = k_gain.astype(jnp.float32)

    def query_part(unnormed_rows, norm_gain):
        return head_norm_rotary(unnormed_rows, norm_gain, cosine_table, sine_table, QUERY_HEADS)

    def key_part(unnormed_rows, norm_gain):
        return head_norm_rotary(unnormed_rows, norm_gain, cosine_table, sine_table, KEY_VALUE_HEADS)

    query_rows = query_part(query_raw, gain_query).astype(jnp.bfloat16)
    key_rows = key_part(key_unnormed, gain_key).astype(jnp.bfloat16)
    value_rows = value_raw.astype(jnp.bfloat16)
    query_four_axes = query_rows.reshape(token_rows, KEY_VALUE_HEADS, queries_per_group, HEAD_SIZE)

    def scores_for(key_rows_part):
        total_amount = key_rows_part.shape[0]
        key_three_axes = key_rows_part.reshape(total_amount, KEY_VALUE_HEADS, HEAD_SIZE)
        scores = (
            jnp.einsum(
                "qhgd,khd->hgqk",
                query_four_axes,
                key_three_axes,
                preferred_element_type=jnp.float32,
            )
            * score_scale
        )
        key_places = jnp.concatenate(
            [
                (my_index ^ part) * token_rows + jnp.arange(token_rows, dtype=jnp.int32)
                for part in range(seq_parts)
            ]
        )
        doc_ends = jnp.cumsum(doc_lengths[0])
        key_segments = jnp.sum((key_places[:, None] >= doc_ends[None, :]).astype(jnp.int32), axis=1)
        allowed = (own_segments[:, None] == key_segments[None, :]) & (
            own_places[:, None] >= key_places[None, :]
        )
        return (scores, allowed, key_three_axes)

    starting_maximum = jnp.full(
        (KEY_VALUE_HEADS, queries_per_group, token_rows), masked_fill_value, jnp.float32
    )
    row_top = starting_maximum
    both_rows = jnp.concatenate(
        gather_seq(jnp.concatenate([key_rows, value_rows], axis=1)), axis=0
    )
    key_rows_part = both_rows[:, :kv_cols]
    value_rows_part = both_rows[:, kv_cols:]
    total_amount = key_rows_part.shape[0]
    scores, allowed, key_three_axes = scores_for(key_rows_part)
    masked = jnp.where(allowed, scores, masked_fill_value)
    new_top = jnp.maximum(row_top, jnp.max(masked, axis=-1))
    expo = jnp.where(allowed, jnp.exp(masked - new_top[..., None]), 0.0)
    row_sum = jnp.sum(expo, axis=-1)
    value_three_axes = value_rows_part.reshape(total_amount, KEY_VALUE_HEADS, HEAD_SIZE)
    summed = jnp.einsum(
        "hgqk,khd->hgqd",
        expo.astype(jnp.bfloat16),
        value_three_axes,
        preferred_element_type=jnp.float32,
    )
    row_top, row_sum, summed = (new_top, row_sum, summed)
    attended = summed / row_sum[..., None]
    log_total = row_top + jnp.log(row_sum)
    attended_b = (
        attended.transpose(2, 0, 1, 3)
        .reshape(token_rows, QUERY_HEADS * HEAD_SIZE)
        .astype(jnp.bfloat16)
    )
    middle = inputs + matmul(attended_b, out_all)
    gain_two = norm2_all.astype(jnp.float32)
    normed2 = rms_scale(middle, gain_two).astype(jnp.bfloat16)
    normed2_all = jnp.concatenate(gather_seq(normed2), axis=0)
    gate_up_pre = matmul(normed2_all, gate_up)
    gate_pre = gate_up_pre[:, :units]
    up_pre = gate_up_pre[:, units:]

    def swiglu(gate_in, up_in):
        return jax.nn.silu(gate_in) * up_in

    swiglu_out, swiglu_pull = jax.vjp(swiglu, gate_pre, up_pre)
    hidden = swiglu_out.astype(jnp.bfloat16)
    d_hidden = contract_cols(grad_all, down_all)
    d_gate, d_up = swiglu_pull(d_hidden)
    gate_up_grads = jnp.concatenate([d_gate.astype(jnp.bfloat16), d_up.astype(jnp.bfloat16)], axis=1)
    d_normed2 = contract_cols(gate_up_grads, gate_up)
    d_normed2 = scatter_seq(jnp.split(d_normed2, seq_parts, axis=0))
    branch = scatter_seq(jnp.split(matmul(hidden, down_all), seq_parts, axis=0))
    block_out = (middle + branch).astype(jnp.bfloat16)
    down_sum = column_term(hidden, grad_all).astype(jnp.bfloat16)
    gate_up_sum = (
        column_term(normed2_all, gate_up_grads)
        .astype(jnp.bfloat16)
        .reshape(dp_parts, seq_parts, fsdp_parts, weight_rows, 2 * units)
        .transpose(0, 2, 1, 3, 4)
        .reshape(MODEL_WIDTH, 2 * units)
    )
    d_normed2, down_sum, gate_up_sum = lax.optimization_barrier((d_normed2, down_sum, gate_up_sum))
    down_sum = lax.psum_scatter(
        down_sum, ("dp", "fsdp"), scatter_dimension=0, tiled=True
    ).astype(jnp.float32)
    gate_up_sum = lax.psum_scatter(gate_up_sum, ("dp", "fsdp"), scatter_dimension=0, tiled=True)
    gate_up_sum = lax.all_to_all(
        gate_up_sum.reshape(seq_parts, weight_rows, 2 * units), "seq", 0, 0
    )

    def to_columns(owned):
        split = owned.reshape(seq_parts, weight_rows, dp_parts, fsdp_parts, unit_rows)
        return split.transpose(1, 2, 0, 3, 4).reshape(weight_rows, FF).astype(jnp.float32)

    grad_gate = to_columns(gate_up_sum[:, :, :units])
    grad_up = to_columns(gate_up_sum[:, :, units:])
    grad_rows = out_grad[0]
    grad_float = grad_rows.astype(jnp.float32)
    norm2_out, norm2_pull = jax.vjp(rms_scale, middle, gain_two)
    d_middle_norm, d_gain_two = norm2_pull(d_normed2)
    d_middle = grad_float + d_middle_norm
    d_branch = d_middle.astype(jnp.bfloat16)
    attended_gradient = contract_cols(d_branch, out_all).astype(jnp.bfloat16)
    attended_grad_four = attended_gradient.reshape(
        token_rows, KEY_VALUE_HEADS, queries_per_group, HEAD_SIZE
    ).transpose(1, 2, 0, 3)
    delta_rows = jnp.sum(attended_grad_four.astype(jnp.float32) * attended, axis=-1)
    scores, allowed, key_three_axes = scores_for(key_rows_part)
    probs = jnp.where(allowed, jnp.exp(scores - log_total[..., None]), 0.0)
    value_three_axes = value_rows_part.reshape(total_amount, KEY_VALUE_HEADS, HEAD_SIZE)
    value_gradient = jnp.einsum(
        "hgqk,hgqd->khd",
        probs.astype(jnp.bfloat16),
        attended_grad_four,
        preferred_element_type=jnp.float32,
    )
    d_probs = jnp.einsum(
        "hgqd,khd->hgqk", attended_grad_four, value_three_axes, preferred_element_type=jnp.float32
    )
    d_scores = (probs * (d_probs - delta_rows[..., None])).astype(jnp.bfloat16)
    d_query_acc = (
        jnp.einsum("hgqk,khd->hgqd", d_scores, key_three_axes, preferred_element_type=jnp.float32)
        * score_scale
    )
    local_key_gradient = (
        jnp.einsum("hgqk,qhgd->khd", d_scores, query_four_axes, preferred_element_type=jnp.float32)
        * score_scale
    )
    every_key_gradient = local_key_gradient.reshape(total_amount, KEY_VALUE_HEADS * HEAD_SIZE)
    every_value_gradient = value_gradient.reshape(total_amount, KEY_VALUE_HEADS * HEAD_SIZE)
    d_both_own = scatter_seq(
        jnp.split(
            jnp.concatenate([every_key_gradient, every_value_gradient], axis=1), seq_parts, axis=0
        )
    ).astype(jnp.bfloat16)
    d_keys_own = d_both_own[:, :kv_cols].astype(jnp.float32)
    d_values_own = d_both_own[:, kv_cols:]
    d_query_rows = rounded(
        d_query_acc.transpose(2, 0, 1, 3).reshape(token_rows, QUERY_HEADS * HEAD_SIZE)
    )
    query_out, query_pull = jax.vjp(query_part, query_raw, gain_query)
    d_query_raw, d_gain_query = query_pull(d_query_rows)
    key_out, key_pull = jax.vjp(key_part, key_unnormed, gain_key)
    d_key_raw, d_gain_key = key_pull(d_keys_own)
    d_query_b = d_query_raw.astype(jnp.bfloat16)
    d_key_b = d_key_raw.astype(jnp.bfloat16)
    projection_grads = jnp.concatenate([d_query_b, d_key_b, d_values_own], axis=1)
    attention_sum = jnp.concatenate(
        [column_term(normed1, projection_grads), column_term(attended_b, d_branch)], axis=1
    ).astype(jnp.bfloat16)
    attention_cols = attention_sum.shape[1]
    attention_sum = attention_sum.reshape(
        dp_parts, seq_parts, fsdp_parts * weight_rows, attention_cols
    )
    attention_sum = scatter_seq(
        [
            lax.dynamic_index_in_dim(attention_sum, my_index ^ part, axis=1, keepdims=False)
            for part in range(seq_parts)
        ]
    ).astype(jnp.bfloat16)
    attention_sum = attention_sum.reshape(dp_parts * fsdp_parts * weight_rows, attention_cols)
    d_normed1 = contract_cols(projection_grads, qkv_all)
    norm1_out, norm1_pull = jax.vjp(rms_scale, inputs, gain_one)
    d_input_norm, d_gain_one = norm1_pull(d_normed1)
    attention_sum, d_gain_one, d_gain_two, d_gain_query, d_gain_key = lax.optimization_barrier(
        (attention_sum, d_gain_one, d_gain_two, d_gain_query, d_gain_key)
    )
    attention_sum = lax.psum_scatter(
        attention_sum, ("dp", "fsdp"), scatter_dimension=0, tiled=True
    ).astype(jnp.float32)
    projection_sum = attention_sum[:, :qkv_cols]
    out_sum = attention_sum[:, qkv_cols:]
    gain_sums = lax.psum((d_gain_one, d_gain_two, d_gain_query, d_gain_key), ("dp", "seq", "fsdp"))
    input_grad = (d_middle + d_input_norm).astype(jnp.bfloat16)
    width_share = weight_rows
    share_start = lax.axis_index(("dp", "seq", "fsdp")) * width_share
    gain_one_own = lax.dynamic_slice_in_dim(gain_sums[0], share_start, width_share)
    gain_two_own = lax.dynamic_slice_in_dim(gain_sums[1], share_start, width_share)
    grad_query = projection_sum[:, :query_cols]
    grad_key = projection_sum[:, query_cols : query_cols + kv_cols]
    grad_value = projection_sum[:, query_cols + kv_cols :]
    return (
        block_out[None],
        input_grad[None],
        gain_one_own,
        grad_query,
        grad_key,
        grad_value,
        out_sum,
        gain_sums[2],
        gain_sums[3],
        gain_two_own,
        grad_gate,
        grad_up,
        down_sum,
    )


def solution(mesh):
    in_specs = (
        P(("dp", "fsdp"), "seq", None),
        P(("dp", "fsdp"), "seq", None),
        P(("dp", "fsdp"), None),
        P(("dp", "fsdp"), "seq"),
        P(("dp", "seq", "fsdp")),
        P(("dp", "seq", "fsdp"), None),
        P(("dp", "seq", "fsdp"), None),
        P(("dp", "seq", "fsdp"), None),
        P(("dp", "seq", "fsdp"), None),
        P(),
        P(),
        P(("dp", "seq", "fsdp")),
        P(("dp", "seq", "fsdp"), None),
        P(("dp", "seq", "fsdp"), None),
        P(("dp", "seq", "fsdp"), None),
    )
    out_specs = (
        P(("dp", "fsdp"), "seq", None),
        P(("dp", "fsdp"), "seq", None),
        P(("dp", "seq", "fsdp")),
        P(("dp", "seq", "fsdp"), None),
        P(("dp", "seq", "fsdp"), None),
        P(("dp", "seq", "fsdp"), None),
        P(("dp", "seq", "fsdp"), None),
        P(),
        P(),
        P(("dp", "seq", "fsdp")),
        P(("dp", "seq", "fsdp"), None),
        P(("dp", "seq", "fsdp"), None),
        P(("dp", "seq", "fsdp"), None),
    )
    return jax.shard_map(body, mesh=mesh, in_specs=in_specs, out_specs=out_specs, check_vma=False)
```
